32 devices in a mesh: gx: 8 (over z, core), gy: 4 (over y, x).
Axes of the slice: x: 2, y: 2, z: 4, core: 2. Of those that a mesh axis runs over, the one named last changes fastest.
Arguments:
- leaf_map: float32 [8, 4, 512, 512], P('gx', 'gy'), may hold values from -0.97 to 0.97, as said below
- source_trace: float32 [8, 4, 512], P('gx', 'gy'), may hold values from -6 to 6
- tile_class: int32 [8, 4, 16], P('gx', 'gy'), may hold values from 0 to 7
- absorb_table: float32 [8], replicated, may hold values from 0.2 to 2
Outputs:
- top_map: float32 [8, 4, 192, 1536], P('gx', 'gy')
- top_out: float32 [8, 4, 192], P('gx', 'gy')
The draws below stay inside these ranges and needn't reach their ends.
Inputs may be any that keep to these rules, and one draw needn't show every extreme that they name: `leaf_map`: each leaf map is a dense matrix whose largest singular value is at most 0.97.
All inputs are finite; a program needn't handle non-finite values.
Results may differ from the reference program's by a relative error of at most 0.000086.
Values sent between devices are 32-bit elements; how exact they have to be, the bound alone decides.
A program may use at most 128 MiB of HBM per device.

```python
import math
import jax
import jax.numpy as jnp
from jax import lax

S = 128
SEG = 32
NCLASS = 8
BOXES_X = 8
BOXES_Y = 4
NSEG = 16
TOP = 1536
ROWS = 192


def orthogonal_draw(key, points):
    normal_block = jax.random.normal(key, (BOXES_X, BOXES_Y, points, points), jnp.float32)
    factor_q, factor_r = jnp.linalg.qr(normal_block)
    diagonal_r = jnp.diagonal(factor_r, axis1=-2, axis2=-1)
    signs = jnp.where(diagonal_r >= 0.0, 1.0, -1.0).astype(jnp.float32)
    return factor_q * signs[..., None, :]


def draw_leaf_map(key, part):
    points = 4 * S
    left_q = orthogonal_draw(jax.random.fold_in(key, 11), points)
    right_q = orthogonal_draw(jax.random.fold_in(key, 12), points)
    uniform_s = jax.random.uniform(jax.random.fold_in(key, 13), (BOXES_X, BOXES_Y, 1, points), jnp.float32, 0.0, 1.0)
    singular = 0.85 + 0.12 * uniform_s
    return jnp.matmul(left_q * singular, right_q, precision=lax.Precision.HIGHEST)


def touch_ends(drawn, rng, low, high):
    longest = drawn.shape.index(max(drawn.shape))
    spots = []
    for shift in (0, 1):
        where = [jax.random.randint(jax.random.fold_in(rng, axis), (), 0, length) for axis, length in enumerate(drawn.shape)]
        where[longest] = (where[longest] + shift) % drawn.shape[longest]
        spots.append(tuple(where))
    return drawn.at[spots[0]].set(low).at[spots[1]].set(high)


def block_levels(stream_key, dims, split, least, largest):
    loudness = 1.0
    for axis_at, shards_of in split:
        steps = jax.random.uniform(jax.random.fold_in(jax.random.fold_in(stream_key, 6), axis_at), (shards_of,), jnp.float32, least / len(split), largest / len(split))
        loudness = loudness * jnp.repeat(jnp.exp(steps), dims[axis_at] // shards_of).reshape((-1,) + (1,) * (len(dims) - 1 - axis_at))
    return loudness


def normal_values(stream_key, shape, width, most, shards=(), kind=jnp.bfloat16):
    values = width * jax.random.normal(stream_key, shape, jnp.float32)
    if shards:
        values = values * block_levels(stream_key, shape, shards, -0.22, 0.18)
    return jnp.clip(values, -most, most).astype(kind)


def setup_inputs(seed: int = 0) -> dict:
    arg_keys = jax.random.split(jax.random.key(seed), 5)
    return {
        "leaf_map": draw_leaf_map(jax.random.fold_in(arg_keys[4], 71), 0),
        "source_trace": normal_values(arg_keys[1], (BOXES_X, BOXES_Y, 4 * S), 1.0, 6.0, ((0, 8), (1, 4)), jnp.float32),
        "tile_class": touch_ends(jax.random.randint(arg_keys[2], (BOXES_X, BOXES_Y, NSEG), 0, NCLASS), jax.random.fold_in(arg_keys[2], 1), 0, NCLASS - 1).astype(jnp.int32),
        "absorb_table": jnp.clip(jnp.exp(jax.random.uniform(arg_keys[3], (NCLASS,), jnp.float32, math.log(0.2), math.log(2.0))), 0.2, 2.0),
    }


precise = lax.Precision.HIGHEST

def matmul_hi(left, right):
    return jnp.matmul(left, right, precision=precise)

def apply_vec(matrix, vector):
    return matmul_hi(matrix, vector[..., None])[..., 0]

def take_rows(matrix, spans):
    return jnp.concatenate([matrix[..., offset:offset + length, :] for offset, length in spans], axis=-2)

def take_cols(matrix, spans):
    return jnp.concatenate([matrix[..., offset:offset + length] for offset, length in spans], axis=-1)

def interface_solve(first_ie, first_ii, second_ie, second_ii, first_hi, second_hi):
    size_int = first_ii.shape[-1]
    coupling = jnp.eye(size_int, dtype=first_ii.dtype) - matmul_hi(first_ii, second_ii)
    right_side = jnp.concatenate([first_ie, -matmul_hi(first_ii, second_ie), (first_hi - apply_vec(first_ii, second_hi))[..., None]], axis=-1)
    coupling_t = jnp.swapaxes(coupling, -1, -2)
    factor = jnp.linalg.cholesky(matmul_hi(coupling_t, coupling))
    solved = jax.scipy.linalg.cho_solve((factor, True), matmul_hi(coupling_t, right_side))
    across = solved[..., :-1]
    across_h = solved[..., -1]
    beyond = jnp.concatenate([jnp.zeros_like(first_ie), second_ie], axis=-1) - matmul_hi(second_ii, across)
    beyond_h = second_hi - apply_vec(second_ii, across_h)
    return (across, across_h, beyond, beyond_h)

def merge_boxes(first_map, first_h, second_map, second_h, first_ext, first_int, second_ext, second_int):
    first_rows = take_rows(first_map, first_ext)
    first_irow = take_rows(first_map, first_int)
    second_rows = take_rows(second_map, second_ext)
    second_irow = take_rows(second_map, second_int)
    across, across_h, beyond, beyond_h = interface_solve(take_cols(first_irow, first_ext), take_cols(first_irow, first_int), take_cols(second_irow, second_ext), take_cols(second_irow, second_int), take_cols(first_h, first_int), take_cols(second_h, second_int))
    own_first = take_cols(first_rows, first_ext)
    link_first = take_cols(first_rows, first_int)
    own_second = take_cols(second_rows, second_ext)
    link_second = take_cols(second_rows, second_int)
    upper = jnp.concatenate([own_first, jnp.zeros(own_first.shape[:-1] + (own_second.shape[-1],), own_first.dtype)], axis=-1) - matmul_hi(link_first, beyond)
    lower = jnp.concatenate([jnp.zeros(own_second.shape[:-1] + (own_first.shape[-1],), own_second.dtype), own_second], axis=-1) - matmul_hi(link_second, across)
    merged = jnp.concatenate([upper, lower], axis=-2)
    merged_h = jnp.concatenate([take_cols(first_h, first_ext) - apply_vec(link_first, beyond_h), take_cols(second_h, second_ext) - apply_vec(link_second, across_h)], axis=-1)
    return (merged, merged_h)

def reorder(matrix, vector, order, unit):
    spans = [(position * unit, unit) for position in order]
    return (take_cols(take_rows(matrix, spans), spans), take_cols(vector, spans))

def reference(leaf_map, source_trace, tile_class, absorb_table):
    levels = absorb_table[tile_class]
    leaf_h = jnp.repeat(levels, SEG, axis=-1) * source_trace
    map1, h1 = merge_boxes(leaf_map[0::2], leaf_h[0::2], leaf_map[1::2], leaf_h[1::2], [(0, S), (2 * S, 2 * S)], [(S, S)], [(S, 3 * S)], [(0, S)])
    map1, h1 = reorder(map1, h1, [0, 3, 1, 4, 2, 5], S)
    map2, h2 = merge_boxes(map1[:, 0::2], h1[:, 0::2], map1[:, 1::2], h1[:, 1::2], [(0, 4 * S)], [(4 * S, 2 * S)], [(0, 2 * S), (4 * S, 2 * S)], [(2 * S, 2 * S)])
    map2, h2 = reorder(map2, h2, [0, 4, 1, 5, 2, 3, 6, 7], S)
    map3, h3 = merge_boxes(map2[0::2], h2[0::2], map2[1::2], h2[1::2], [(0, 2 * S), (4 * S, 4 * S)], [(2 * S, 2 * S)], [(2 * S, 6 * S)], [(0, 2 * S)])
    blocks = [h3[..., k * 2 * S:(k + 1) * 2 * S] for k in range(6)]
    zero_x = jnp.zeros_like(blocks[0][:1])
    from_west = jnp.concatenate([zero_x, blocks[3][:-1]], axis=0)
    from_east = jnp.concatenate([blocks[0][1:], zero_x], axis=0)
    north_edge = jnp.concatenate([blocks[2], blocks[5]], axis=-1)
    south_edge = jnp.concatenate([blocks[1], blocks[4]], axis=-1)
    zero_y = jnp.zeros_like(north_edge[:, :1])
    from_south = jnp.concatenate([zero_y, north_edge[:, :-1]], axis=1)
    from_north = jnp.concatenate([south_edge[:, 1:], zero_y], axis=1)
    incoming = -jnp.concatenate([from_west, from_south[..., :2 * S], from_north[..., :2 * S], from_east, from_south[..., 2 * S:], from_north[..., 2 * S:]], axis=-1)
    outgoing = apply_vec(map3, incoming) + h3
    tops_x = map3.shape[0]
    tops_y = map3.shape[1]
    scaled = map3 * math.sqrt(TOP)
    top_map = scaled.reshape(tops_x, tops_y, 4, 2, ROWS, TOP).transpose(0, 2, 1, 3, 4, 5).reshape(tops_x * 4, tops_y * 2, ROWS, TOP)
    top_out = outgoing.reshape(tops_x, tops_y, 4, 2, ROWS).transpose(0, 2, 1, 3, 4).reshape(tops_x * 4, tops_y * 2, ROWS)
    return (top_map, top_out)
```

```python
import functools
import math

import jax
import jax.numpy as jnp
from jax import lax
from jax.experimental import pallas as pl
from jax.experimental.pallas import tpu as pltpu
from jax.sharding import PartitionSpec as P

DOUBLINGS = 9


def split(value):
    high = value.astype(jnp.bfloat16)
    low = (value - high.astype(jnp.float32)).astype(jnp.bfloat16)
    return high, low


def dot_parts(left, right):
    dot = functools.partial(jnp.dot, preferred_element_type=jnp.float32)
    return dot(left[0], right[0]) + (dot(left[0], right[1]) + dot(left[1], right[0]))


def dot3(left, right):
    return dot_parts(split(left), split(right))


def resolvent(product):
    size = product.shape[0]
    rows = lax.broadcasted_iota(jnp.int32, (size, size), 0)
    cols = lax.broadcasted_iota(jnp.int32, (size, size), 1)
    total = jnp.where(rows == cols, 1.0, 0.0) + product
    parts = split(product)
    power = dot_parts(parts, parts)
    for step in range(1, DOUBLINGS):
        parts = split(power)
        if step < DOUBLINGS - 1:
            sums = split(total)
            both = tuple(jnp.concatenate([s, p], axis=0) for s, p in zip(sums, parts))
            out = dot_parts(both, parts)
            total = total + out[:size]
            power = out[size:]
        else:
            total = total + dot_parts(split(total), parts)
    return total


def as_columns(row):
    return jnp.broadcast_to(row, (128, row.shape[1])).T


def gain(t_ii, o_ii, o_ri, t_h, o_h):
    t_parts = split(t_ii)
    inverse = resolvent(dot_parts(t_parts, split(o_ii)))
    g = dot3(o_ri, inverse)
    gt = dot_parts(split(g), t_parts)
    jump = as_columns(t_h) - dot_parts(t_parts, split(as_columns(o_h)))
    change = dot3(g, jump)
    short = -change.shape[0] % 128
    if short:
        change = jnp.concatenate([change, jnp.zeros((short, 128), jnp.float32)], axis=0)
    return g, gt, change.T[0:1, :]


def ordered(flag, mine, other):
    return jnp.concatenate(
        [jnp.where(flag, mine, other), jnp.where(flag, other, mine)], axis=0
    )


def kernel1(flags, own, other, h, other_h, re, ri, ie, ii, h_out):
    left, low = flags[0] == 1, flags[1] == 1
    s = own.shape[0] // 4
    e = 3 * s
    g, gt, change = gain(
        other[:, e:], own[e:, e:], own[:e, e:], other_h[...], h[:, e:]
    )
    mine = own[:e, :e] + dot3(gt, own[e:, :e])
    cross = -dot3(g, other[:, :e])
    h_new = h[:, :e] - change
    lefts = jnp.where(left, mine, cross)
    rights = jnp.where(left, cross, mine)

    def col(block, k):
        return block[:, k * s : (k + 1) * s]

    def rows(block):
        x, south, north = block[:s], block[s : 2 * s], block[2 * s :]
        return x, jnp.where(low, south, north), jnp.where(low, north, south)

    def put(k, side):
        x, y, i = rows(side)
        re[0:s, k * s : (k + 1) * s] = x
        re[s : 2 * s, k * s : (k + 1) * s] = y
        ie[:, k * s : (k + 1) * s] = i

    def put_i(k, side):
        x, y, i = rows(side)
        ri[0:s, k * s : (k + 1) * s] = x
        ri[s : 2 * s, k * s : (k + 1) * s] = y
        ii[0:s, k * s : (k + 1) * s] = i

    put(0, col(lefts, 0))
    put(1, col(rights, 0))
    for k, side in enumerate((lefts, rights)):
        put(2 + k, jnp.where(low, col(side, 1), col(side, 2)))
        put_i(k, jnp.where(low, col(side, 2), col(side, 1)))
    hx, hs, hn = col(h_new, 0), col(h_new, 1), col(h_new, 2)
    h_out[:, 0:s] = hx
    h_out[:, s : 2 * s] = jnp.where(low, hs, hn)
    hi = jnp.where(low, hn, hs)
    ii[s:, :] = jnp.broadcast_to(jnp.concatenate([hi, hi], axis=1), (8, 2 * s))


def gain2(flags, mine, mine_o, t, t_o, ri, h, g, gt, h_out):
    left = flags[0] == 1
    s = mine.shape[0] - 8

    def both(a, b):
        rows = ordered(left, a[0:s, :], b[0:s, :])
        ha, hb = a[s : s + 1, 0:s], b[s : s + 1, 0:s]
        vec = jnp.concatenate(
            [jnp.where(left, ha, hb), jnp.where(left, hb, ha)], axis=1
        )
        return rows, vec

    o_ii, o_h = both(mine, mine_o)
    t_ii, t_h = both(t, t_o)
    g[...], gt[...], change = gain(t_ii, o_ii, ri[...], t_h, o_h)
    h_out[...] = h[...] - change


def apply2(flags, re, g, gt, mine, mine_o, t, t_o, ext, inner):
    left, low, first = flags[0] == 1, flags[1] == 1, flags[2] == 1
    s = mine.shape[0]
    own = re[...] + dot3(gt[...], ordered(left, mine[...], mine_o[...]))
    cross = -dot3(g[...], ordered(left, t[...], t_o[...]))
    lows = jnp.where(low, own, cross)
    ups = jnp.where(low, cross, own)
    west = jnp.concatenate([lows[:, :s], ups[:, :s]], axis=1)
    east = jnp.concatenate([lows[:, s : 2 * s], ups[:, s : 2 * s]], axis=1)
    ext[:, : 2 * s] = jnp.where(first, west, east)
    ext[:, 2 * s : 4 * s] = lows[:, 2 * s :]
    ext[:, 4 * s :] = ups[:, 2 * s :]
    inner[...] = jnp.where(first, east, west)


def quads(flags, mine, other, n):
    left, low = flags[0] == 1, flags[1] == 1
    a = ordered(left, mine[0], other[0])
    b = ordered(left, mine[1], other[1])
    return ordered(low, a, b)


def gain3(flags, mine, other, far, far_o, ri, g, gt, change):
    low = flags[1] == 1
    n = mine.shape[1] - 8

    def both(a, b):
        rows = quads(flags, (a[0, 0:n, :], a[1, 0:n, :]), (b[0, 0:n, :], b[1, 0:n, :]), n)
        h0, h1 = a[0, n : n + 1, 0 : 2 * n], a[1, n : n + 1, 0 : 2 * n]
        vec = jnp.concatenate(
            [jnp.where(low, h0, h1), jnp.where(low, h1, h0)], axis=1
        )
        return rows, vec

    o_ii, o_h = both(mine, other)
    t_ii, t_h = both(far, far_o)
    g[...], gt[...], change[...] = gain(t_ii, o_ii, ri[...], t_h, o_h)


def apply3(scale, flags, re, g, gt, mine, other, far, far_o, out):
    first = flags[2] == 1
    n = mine.shape[1]
    e = re.shape[1]
    o_ie = quads(flags, (mine[0], mine[1]), (other[0], other[1]), n)
    t_ie = quads(flags, (far[0], far[1]), (far_o[0], far_o[1]), n)
    own = (re[...] + dot3(gt[...], o_ie)) * scale
    cross = dot3(g[...], t_ie) * (-scale)
    out[:, :e] = jnp.where(first, own, cross)
    out[:, e:] = jnp.where(first, cross, own)


def call(body, flags, operands, shapes, flops):
    outs = [jax.ShapeDtypeStruct(shape, jnp.float32) for shape in shapes]
    moved = 4 * sum(math.prod(a.shape) for a in list(operands) + outs)
    return pl.pallas_call(
        body,
        out_shape=outs,
        in_specs=[pl.BlockSpec(memory_space=pltpu.SMEM)]
        + [pl.BlockSpec(memory_space=pltpu.VMEM)] * len(operands),
        out_specs=[pl.BlockSpec(memory_space=pltpu.VMEM)] * len(outs),
        compiler_params=pltpu.CompilerParams(vmem_limit_bytes=40 * 2**20),
        cost_estimate=pl.CostEstimate(flops=flops, bytes_accessed=moved, transcendentals=0),
    )(flags, *operands)


def from_behind(block, axis, distance):
    devices = range(lax.axis_size(axis))
    route = [(i - distance, i) for i in devices if i - distance in devices]
    return lax.ppermute(block, axis, route)


def partner(value, axis, distance):
    mask = 2**distance
    pairs = [(source, source ^ mask) for source in range(lax.axis_size(axis))]
    return lax.ppermute(value, axis, pairs)


def send(value, moves):
    wide, high = lax.axis_size("gx"), lax.axis_size("gy")
    pairs = []
    for i in range(wide):
        for j in range(high):
            to = moves(i, j)
            if to is not None:
                pairs.append((i * high + j, to[0] * high + to[1]))
    return lax.ppermute(value, ("gx", "gy"), pairs)


def local(leaf_map, source_trace, tile_class, absorb_table):
    leaf_op = leaf_map[0, 0]
    s = leaf_op.shape[0] // 4
    classes = tile_class[0, 0]
    chosen = (
        classes[:, None] == jnp.arange(absorb_table.shape[0], dtype=jnp.int32)[None, :]
    ).astype(jnp.float32)
    levels = jnp.sum(chosen * absorb_table[None, :], axis=1)
    seg_width = leaf_op.shape[0] // classes.shape[0]
    spread = jnp.broadcast_to(levels[:, None], (classes.shape[0], seg_width)).reshape(-1)
    leaf_h = spread * source_trace[0, 0]
    column = lax.axis_index("gx")
    row_index = lax.axis_index("gy")
    left = column % 2 == 0
    low = row_index % 2 == 0
    first = column // 2 % 2 == 0
    flags = jnp.stack([left, low, first]).astype(jnp.int32)

    def sides(a, axis):
        w, e, so, no = jnp.split(a, 4, axis=axis)
        x, i = jnp.where(left, w, e), jnp.where(left, e, w)
        return jnp.concatenate([x, so, no, i], axis=axis)

    own = sides(sides(leaf_op, 0), 1)
    h = sides(leaf_h, 0)[None]
    other, other_h = partner((own[3 * s :], h[:, 3 * s :]), "gx", 0)
    re, ri, ie, ii, h = call(
        kernel1,
        flags,
        [own, other, h, other_h],
        [(2 * s, 4 * s), (2 * s, 2 * s), (s, 4 * s), (s + 8, 2 * s), (1, 2 * s)],
        6 * s**3 * 50,
    )

    t_ii = partner(ii, "gy", 0)
    ii_o = partner(ii, "gx", 0)
    t_ii_o = partner(t_ii, "gx", 0)
    t_ie = partner(ie, "gy", 0)
    ie_o = partner(ie, "gx", 0)
    t_ie_o = partner(t_ie, "gx", 0)
    g, gt, h = call(
        gain2,
        flags,
        [ii, ii_o, t_ii, t_ii_o, ri, h],
        [(2 * s, 2 * s), (2 * s, 2 * s), (1, 2 * s)],
        6 * (2 * s) ** 3 * 20,
    )
    ext, inner = call(
        apply2,
        flags,
        [re, g, gt, ie, ie_o, t_ie, t_ie_o],
        [(2 * s, 6 * s), (2 * s, 2 * s)],
        6 * (2 * s) ** 2 * 8 * s,
    )

    half = s // 2
    x_i, x_e = inner[:s], ext[:s]
    to_first = lambda a: jnp.where(left, a[half:], a[:half])
    keep = lambda a: jnp.where(left, a[:half], a[half:])
    holder = left != first

    def give(i, j):
        return (i ^ 1, j) if (i % 2 == 0) != (i // 2 % 2 == 0) else None

    h_x = jnp.broadcast_to(jnp.concatenate([h[:, :s], h[:, :s]], axis=1), (8, 2 * s))
    got_i = send(jnp.concatenate([to_first(x_i), h_x], axis=0), give)
    got_e = send(to_first(x_e), give)
    v_i = jnp.where(holder, jnp.concatenate([keep(x_i), h_x], axis=0), got_i)
    v_e = jnp.where(holder, keep(x_e), got_e)

    mine_i = jnp.stack([v_i, partner(v_i, "gy", 0)])
    far_i = partner(mine_i, "gx", 1)
    mine_i_o = partner(mine_i, "gx", 0)
    far_i_o = partner(far_i, "gx", 0)
    mine_e = jnp.stack([v_e, partner(v_e, "gy", 0)])
    far_e = partner(mine_e, "gx", 1)
    mine_e_o = partner(mine_e, "gx", 0)
    far_e_o = partner(far_e, "gx", 0)

    def in_first(i):
        return i // 2 % 2 == 0

    def move_a(i, j):
        if i % 2 == 0 and j % 2 == 0:
            return (i, j + 1)
        if i % 2 == 1 and j % 2 == 0 and not in_first(i):
            return (i - 1, j)
        return None

    def move_b(i, j):
        if j % 2 == 1 and i % 2 == (0 if in_first(i) else 1):
            return (i - i % 2, j - 1)
        return None

    def move_c(i, j):
        return (i + 1, j - 1) if i % 2 == 0 and j % 2 == 1 else None

    def move_d(i, j):
        if j % 2 == 1 and (i % 2 == 0 or not in_first(i)):
            return (i ^ 1, j)
        return None

    def rows_of(a):
        x, y = a[:s], a[s:]
        got_a = send(jnp.where(left, y, x), move_a)
        got_b = send(x[:half], move_b)
        got_c = send(y[:half], move_c)
        got_d = send(jnp.where(left, y[half:], x[half:]), move_d)
        lower = jnp.where(
            left,
            jnp.concatenate([jnp.where(first, x, got_a), got_b], axis=0),
            jnp.concatenate([y, got_c], axis=0),
        )
        upper = jnp.where(
            left,
            jnp.concatenate([jnp.where(first, x[half:], got_d), got_a], axis=0),
            jnp.concatenate([got_d, y], axis=0),
        )
        return jnp.where(low, lower, upper)

    row_i = rows_of(inner)
    row_h = rows_of(h[0])
    row_e = rows_of(ext)
    rows_dev = 3 * s // 2
    g, gt, change = call(
        gain3,
        flags,
        [mine_i, mine_i_o, far_i, far_i_o, row_i],
        [(rows_dev, 2 * s), (rows_dev, 2 * s), (1, 2 * s)],
        6 * (2 * s) ** 3 * 20,
    )
    h3 = row_h - change[0, :rows_dev]
    scale = math.sqrt(12 * s)
    (scaled,) = call(
        functools.partial(apply3, scale),
        flags,
        [row_e, g, gt, mine_e, mine_e_o, far_e, far_e_o],
        [(rows_dev, 12 * s)],
        6 * rows_dev * 2 * s * 12 * s,
    )

    top_h = h3
    for flag, axis, distance in ((low, "gy", 0), (left, "gx", 0), (first, "gx", 1)):
        top_h = ordered(flag, top_h, partner(top_h, axis, distance))
    edge = 2 * s
    blocks = [top_h[k * edge : (k + 1) * edge] for k in range(6)]
    from_west = from_behind(blocks[3], "gx", 4)
    from_east = from_behind(blocks[0], "gx", -4)
    from_south = from_behind(jnp.concatenate([blocks[2], blocks[5]]), "gy", 2)
    from_north = from_behind(jnp.concatenate([blocks[1], blocks[4]]), "gy", -2)
    incoming = -jnp.concatenate(
        [
            from_west,
            from_south[:edge],
            from_north[:edge],
            from_east,
            from_south[edge:],
            from_north[edge:],
        ]
    )
    out_rows = jnp.sum(scaled * (incoming / scale)[None, :], axis=1) + h3
    return (scaled[None, None], out_rows[None, None])


def solution(mesh):
    return jax.shard_map(
        local,
        mesh=mesh,
        in_specs=(P("gx", "gy", None, None), P("gx", "gy", None), P("gx", "gy", None), P()),
        out_specs=(P("gx", "gy", None, None), P("gx", "gy", None)),
        check_vma=False,
    )
```

```python
import functools
import math

import jax
import jax.numpy as jnp
from jax import lax
from jax.experimental import pallas as pl
from jax.experimental.pallas import tpu as pltpu
from jax.sharding import PartitionSpec as P

DOUBLINGS = 9


def split(value):
    high = value.astype(jnp.bfloat16)
    low = (value - high.astype(jnp.float32)).astype(jnp.bfloat16)
    return high, low


def dot_parts(left, right):
    dot = functools.partial(jnp.dot, preferred_element_type=jnp.float32)
    return dot(left[0], right[0]) + (dot(left[0], right[1]) + dot(left[1], right[0]))


def dot3(left, right):
    return dot_parts(split(left), split(right))


def resolvent(product):
    size = product.shape[0]
    rows = lax.broadcasted_iota(jnp.int32, (size, size), 0)
    cols = lax.broadcasted_iota(jnp.int32, (size, size), 1)
    total = jnp.where(rows == cols, 1.0, 0.0) + product
    parts = split(product)
    power = dot_parts(parts, parts)
    for step in range(1, DOUBLINGS):
        parts = split(power)
        if step < DOUBLINGS - 1:
            sums = split(total)
            both = tuple(jnp.concatenate([s, p], axis=0) for s, p in zip(sums, parts))
            out = dot_parts(both, parts)
            total = total + out[:size]
            power = out[size:]
        else:
            total = total + dot_parts(split(total), parts)
    return total


def as_columns(row):
    return jnp.broadcast_to(row, (128, row.shape[1])).T


def gain(t_ii, o_ii, o_ri, t_h, o_h):
    return apply_gain(*interface(t_ii, o_ii, t_h, o_h), t_ii, o_ri)


def interface(t_ii, o_ii, t_h, o_h):
    t_parts = split(t_ii)
    inverse = resolvent(dot_parts(t_parts, split(o_ii)))
    return inverse, as_columns(t_h) - dot_parts(t_parts, split(as_columns(o_h)))


def apply_gain(inverse, jump, t_ii, o_ri):
    g = dot3(o_ri, inverse)
    gt = dot3(g, t_ii)
    change = dot3(g, jump)
    short = -change.shape[0] % 128
    if short:
        change = jnp.concatenate([change, jnp.zeros((short, 128), jnp.float32)], axis=0)
    return g, gt, change.T[0:1, :]


def ordered(flag, mine, other):
    return jnp.concatenate(
        [jnp.where(flag, mine, other), jnp.where(flag, other, mine)], axis=0
    )


def kernel1(flags, own, other, h, other_h, re, ri, ie, ii, h_out):
    left, low = flags[0] == 1, flags[1] == 1
    s = own.shape[0] // 4
    e = 3 * s
    g, gt, change = gain(
        other[:, e:], own[e:, e:], own[:e, e:], other_h[...], h[:, e:]
    )
    mine = own[:e, :e] + dot3(gt, own[e:, :e])
    cross = -dot3(g, other[:, :e])
    h_new = h[:, :e] - change
    lefts = jnp.where(left, mine, cross)
    rights = jnp.where(left, cross, mine)

    def col(block, k):
        return block[:, k * s : (k + 1) * s]

    def rows(block):
        x, south, north = block[:s], block[s : 2 * s], block[2 * s :]
        return x, jnp.where(low, south, north), jnp.where(low, north, south)

    def put(k, side):
        x, y, i = rows(side)
        re[0:s, k * s : (k + 1) * s] = x
        re[s : 2 * s, k * s : (k + 1) * s] = y
        ie[:, k * s : (k + 1) * s] = i

    def put_i(k, side):
        x, y, i = rows(side)
        ri[0:s, k * s : (k + 1) * s] = x
        ri[s : 2 * s, k * s : (k + 1) * s] = y
        ii[0:s, k * s : (k + 1) * s] = i

    put(0, col(lefts, 0))
    put(1, col(rights, 0))
    for k, side in enumerate((lefts, rights)):
        put(2 + k, jnp.where(low, col(side, 1), col(side, 2)))
        put_i(k, jnp.where(low, col(side, 2), col(side, 1)))
    hx, hs, hn = col(h_new, 0), col(h_new, 1), col(h_new, 2)
    h_out[:, 0:s] = hx
    h_out[:, s : 2 * s] = jnp.where(low, hs, hn)
    hi = jnp.where(low, hn, hs)
    ii[s:, :] = jnp.broadcast_to(jnp.concatenate([hi, hi], axis=1), (8, 2 * s))


def gain2(flags, mine, mine_o, t, t_o, ri, h, g, gt, h_out):
    left = flags[0] == 1
    s = mine.shape[0] - 8

    def both(a, b):
        rows = ordered(left, a[0:s, :], b[0:s, :])
        ha, hb = a[s : s + 1, 0:s], b[s : s + 1, 0:s]
        vec = jnp.concatenate(
            [jnp.where(left, ha, hb), jnp.where(left, hb, ha)], axis=1
        )
        return rows, vec

    o_ii, o_h = both(mine, mine_o)
    t_ii, t_h = both(t, t_o)
    g[...], gt[...], change = gain(t_ii, o_ii, ri[...], t_h, o_h)
    h_out[...] = h[...] - change


def apply2(flags, re, g, gt, mine, mine_o, t, t_o, ext, inner):
    left, low, first = flags[0] == 1, flags[1] == 1, flags[2] == 1
    s = mine.shape[0]
    own = re[...] + dot3(gt[...], ordered(left, mine[...], mine_o[...]))
    cross = -dot3(g[...], ordered(left, t[...], t_o[...]))
    lows = jnp.where(low, own, cross)
    ups = jnp.where(low, cross, own)
    west = jnp.concatenate([lows[:, :s], ups[:, :s]], axis=1)
    east = jnp.concatenate([lows[:, s : 2 * s], ups[:, s : 2 * s]], axis=1)
    ext[:, : 2 * s] = jnp.where(first, west, east)
    ext[:, 2 * s : 4 * s] = lows[:, 2 * s :]
    ext[:, 4 * s :] = ups[:, 2 * s :]
    inner[...] = jnp.where(first, east, west)


def quads(flags, mine, other):
    left, low = flags[0] == 1, flags[1] == 1
    a = ordered(left, mine[0], other[0])
    b = ordered(left, mine[1], other[1])
    return ordered(low, a, b)


def solve3(flags, m0, m1, o0, o1, f0, f1, p0, p1, inverse, jump, t_out):
    low = flags[1] == 1
    n = m0.shape[0] - 8

    def both(a, b):
        rows = quads(flags, [r[0:n, :] for r in a], [r[0:n, :] for r in b])
        h0, h1 = a[0][n : n + 1, 0 : 2 * n], a[1][n : n + 1, 0 : 2 * n]
        vec = jnp.concatenate(
            [jnp.where(low, h0, h1), jnp.where(low, h1, h0)], axis=1
        )
        return rows, vec

    o_ii, o_h = both((m0, m1), (o0, o1))
    t_ii, t_h = both((f0, f1), (p0, p1))
    inverse[...], jump[...] = interface(t_ii, o_ii, t_h, o_h)
    t_out[...] = t_ii


def gain3(flags, inverse, jump, t_ii, ri, g, gt, change):
    g[...], gt[...], change[...] = apply_gain(inverse[...], jump[...], t_ii[...], ri[...])


def apply3(scale, flags, re, g, gt, m0, m1, o0, o1, f0, f1, p0, p1, out):
    first = flags[2] == 1
    e = re.shape[1]
    o_ie = quads(flags, (m0[...], m1[...]), (o0[...], o1[...]))
    t_ie = quads(flags, (f0[...], f1[...]), (p0[...], p1[...]))
    own = (re[...] + dot3(gt[...], o_ie)) * scale
    cross = dot3(g[...], t_ie) * (-scale)
    out[:, :e] = jnp.where(first, own, cross)
    out[:, e:] = jnp.where(first, cross, own)


def call(body, flags, operands, shapes, flops):
    outs = [jax.ShapeDtypeStruct(shape, jnp.float32) for shape in shapes]
    moved = 4 * sum(math.prod(a.shape) for a in list(operands) + outs)
    return pl.pallas_call(
        body,
        out_shape=outs,
        in_specs=[pl.BlockSpec(memory_space=pltpu.SMEM)]
        + [pl.BlockSpec(memory_space=pltpu.VMEM)] * len(operands),
        out_specs=[pl.BlockSpec(memory_space=pltpu.VMEM)] * len(outs),
        compiler_params=pltpu.CompilerParams(vmem_limit_bytes=40 * 2**20),
        cost_estimate=pl.CostEstimate(flops=flops, bytes_accessed=moved, transcendentals=0),
    )(flags, *operands)


def from_behind(block, axis, distance):
    devices = range(lax.axis_size(axis))
    route = [(i - distance, i) for i in devices if i - distance in devices]
    return lax.ppermute(block, axis, route)


def partner(value, axis, distance):
    mask = 2**distance
    pairs = [(source, source ^ mask) for source in range(lax.axis_size(axis))]
    return lax.ppermute(value, axis, pairs)


def after(value, earlier):
    return lax.optimization_barrier((value, earlier))[0]


def send(value, moves):
    wide, high = lax.axis_size("gx"), lax.axis_size("gy")
    pairs = []
    for i in range(wide):
        for j in range(high):
            to = moves(i, j)
            if to is not None:
                pairs.append((i * high + j, to[0] * high + to[1]))
    return lax.ppermute(value, ("gx", "gy"), pairs)


def local(leaf_map, source_trace, tile_class, absorb_table):
    leaf_op = leaf_map[0, 0]
    s = leaf_op.shape[0] // 4
    classes = tile_class[0, 0]
    chosen = (
        classes[:, None] == jnp.arange(absorb_table.shape[0], dtype=jnp.int32)[None, :]
    ).astype(jnp.float32)
    levels = jnp.sum(chosen * absorb_table[None, :], axis=1)
    seg_width = leaf_op.shape[0] // classes.shape[0]
    spread = jnp.broadcast_to(levels[:, None], (classes.shape[0], seg_width)).reshape(-1)
    leaf_h = spread * source_trace[0, 0]
    column = lax.axis_index("gx")
    row_index = lax.axis_index("gy")
    left = column % 2 == 0
    low = row_index % 2 == 0
    first = column // 2 % 2 == 0
    flags = jnp.stack([left, low, first]).astype(jnp.int32)

    def sides(a, axis):
        w, e, so, no = jnp.split(a, 4, axis=axis)
        x, i = jnp.where(left, w, e), jnp.where(left, e, w)
        return jnp.concatenate([x, so, no, i], axis=axis)

    own = sides(sides(leaf_op, 0), 1)
    h = sides(leaf_h, 0)[None]
    other, other_h = partner((own[3 * s :], h[:, 3 * s :]), "gx", 0)
    re, ri, ie, ii, h = call(
        kernel1,
        flags,
        [own, other, h, other_h],
        [(2 * s, 4 * s), (2 * s, 2 * s), (s, 4 * s), (s + 8, 2 * s), (1, 2 * s)],
        6 * s**3 * 50,
    )

    t_ii = partner(ii, "gy", 0)
    ii_o = partner(ii, "gx", 0)
    t_ii_o = partner(t_ii, "gx", 0)
    t_ie = partner(after(ie, t_ii), "gy", 0)
    ie_o = partner(ie, "gx", 0)
    t_ie_o = partner(t_ie, "gx", 0)
    g, gt, h = call(
        gain2,
        flags,
        [ii, ii_o, t_ii, t_ii_o, ri, h],
        [(2 * s, 2 * s), (2 * s, 2 * s), (1, 2 * s)],
        6 * (2 * s) ** 3 * 20,
    )
    ext, inner = call(
        apply2,
        flags,
        [re, g, gt, ie, ie_o, t_ie, t_ie_o],
        [(2 * s, 6 * s), (2 * s, 2 * s)],
        6 * (2 * s) ** 2 * 8 * s,
    )

    half = s // 2
    x_i, x_e = inner[:s], ext[:s]
    to_first = lambda a: jnp.where(left, a[half:], a[:half])
    keep = lambda a: jnp.where(left, a[:half], a[half:])
    holder = left != first

    def give(i, j):
        return (i ^ 1, j) if (i % 2 == 0) != (i // 2 % 2 == 0) else None

    h_x = jnp.broadcast_to(jnp.concatenate([h[:, :s], h[:, :s]], axis=1), (8, 2 * s))
    got_i = send(jnp.concatenate([to_first(x_i), h_x], axis=0), give)
    got_e = send(after(to_first(x_e), got_i), give)
    v_i = jnp.where(holder, jnp.concatenate([keep(x_i), h_x], axis=0), got_i)
    v_e = jnp.where(holder, keep(x_e), got_e)

    def spread_out(v):
        beside = partner(v, "gy", 0)
        far = partner(v, "gx", 1)
        far_beside = partner(beside, "gx", 1)
        pieces = [v, beside, far, far_beside]
        shared = [partner(piece, "gx", 0) for piece in pieces]
        return pieces[:2] + shared[:2] + pieces[2:] + shared[2:]

    quad_i = spread_out(v_i)
    quad_e = spread_out(after(v_e, quad_i[5]))

    def in_first(i):
        return i // 2 % 2 == 0

    def move_a(i, j):
        if i % 2 == 0 and j % 2 == 0:
            return (i, j + 1)
        if i % 2 == 1 and j % 2 == 0 and not in_first(i):
            return (i - 1, j)
        return None

    def move_b(i, j):
        if j % 2 == 1 and i % 2 == (0 if in_first(i) else 1):
            return (i - i % 2, j - 1)
        return None

    def move_c(i, j):
        return (i + 1, j - 1) if i % 2 == 0 and j % 2 == 1 else None

    def move_d(i, j):
        if j % 2 == 1 and (i % 2 == 0 or not in_first(i)):
            return (i ^ 1, j)
        return None

    def rows_of(a):
        x, y = a[:s], a[s:]
        got_a = send(jnp.where(left, y, x), move_a)
        got_b = send(x[:half], move_b)
        got_c = send(y[:half], move_c)
        got_d = send(jnp.where(left, y[half:], x[half:]), move_d)
        lower = jnp.where(
            left,
            jnp.concatenate([jnp.where(first, x, got_a), got_b], axis=0),
            jnp.concatenate([y, got_c], axis=0),
        )
        upper = jnp.where(
            left,
            jnp.concatenate([jnp.where(first, x[half:], got_d), got_a], axis=0),
            jnp.concatenate([got_d, y], axis=0),
        )
        return jnp.where(low, lower, upper)

    row_i = rows_of(after(inner, quad_i[1]))
    row_h = rows_of(h[0])
    row_e = rows_of(after(ext, quad_i[5]))
    rows_dev = 3 * s // 2
    solved = call(
        solve3,
        flags,
        quad_i,
        [(2 * s, 2 * s), (2 * s, 128), (2 * s, 2 * s)],
        6 * (2 * s) ** 3 * 40,
    )
    row_i = after(row_i, (quad_e[1], quad_e[4], row_e))
    g, gt, change = call(
        gain3,
        flags,
        [*solved, row_i],
        [(rows_dev, 2 * s), (rows_dev, 2 * s), (1, 2 * s)],
        6 * (2 * s) ** 3 * 2,
    )
    h3 = row_h - change[0, :rows_dev]
    scale = math.sqrt(12 * s)
    (scaled,) = call(
        functools.partial(apply3, scale),
        flags,
        [row_e, g, gt, *quad_e],
        [(rows_dev, 12 * s)],
        6 * rows_dev * 2 * s * 12 * s,
    )

    top_h = h3
    for flag, axis, distance in ((low, "gy", 0), (left, "gx", 0), (first, "gx", 1)):
        top_h = ordered(flag, top_h, partner(top_h, axis, distance))
    edge = 2 * s
    blocks = [top_h[k * edge : (k + 1) * edge] for k in range(6)]
    from_west = from_behind(blocks[3], "gx", 4)
    from_east = from_behind(blocks[0], "gx", -4)
    from_south = from_behind(jnp.concatenate([blocks[2], blocks[5]]), "gy", 2)
    from_north = from_behind(jnp.concatenate([blocks[1], blocks[4]]), "gy", -2)
    from_west, from_east, from_south, from_north = lax.optimization_barrier(
        (from_west, from_east, from_south, from_north)
    )
    incoming = -jnp.concatenate(
        [
            from_west,
            from_south[:edge],
            from_north[:edge],
            from_east,
            from_south[edge:],
            from_north[edge:],
        ]
    )
    out_rows = jnp.sum(scaled * (incoming / scale)[None, :], axis=1) + h3
    return (scaled[None, None], out_rows[None, None])


def solution(mesh):
    return jax.shard_map(
        local,
        mesh=mesh,
        in_specs=(P("gx", "gy", None, None), P("gx", "gy", None), P("gx", "gy", None), P()),
        out_specs=(P("gx", "gy", None, None), P("gx", "gy", None)),
        check_vma=False,
    )
```

```python
import functools
import math

import jax
import jax.numpy as jnp
from jax import lax
from jax.experimental import pallas as pl
from jax.experimental.pallas import tpu as pltpu
from jax.sharding import PartitionSpec as P

DOUBLINGS = 9


def split(value):
    high = value.astype(jnp.bfloat16)
    low = (value - high.astype(jnp.float32)).astype(jnp.bfloat16)
    return high, low


def dot_parts(left, right):
    dot = functools.partial(jnp.dot, preferred_element_type=jnp.float32)
    return dot(left[0], right[0]) + (dot(left[0], right[1]) + dot(left[1], right[0]))


def dot3(left, right):
    return dot_parts(split(left), split(right))


def resolvent(product):
    size = product.shape[0]
    rows = lax.broadcasted_iota(jnp.int32, (size, size), 0)
    cols = lax.broadcasted_iota(jnp.int32, (size, size), 1)
    total = jnp.where(rows == cols, 1.0, 0.0) + product
    parts = split(product)
    power = dot_parts(parts, parts)
    for step in range(1, DOUBLINGS):
        parts = split(power)
        if step < DOUBLINGS - 1:
            sums = split(total)
            both = tuple(jnp.concatenate([s, p], axis=0) for s, p in zip(sums, parts))
            out = dot_parts(both, parts)
            total = total + out[:size]
            power = out[size:]
        else:
            total = total + dot_parts(split(total), parts)
    return total


def as_columns(row):
    return jnp.broadcast_to(row, (128, row.shape[1])).T


def gain(t_ii, o_ii, o_ri, t_h, o_h):
    return apply_gain(*interface(t_ii, o_ii, t_h, o_h), t_ii, o_ri)


def interface(t_ii, o_ii, t_h, o_h):
    t_parts = split(t_ii)
    inverse = resolvent(dot_parts(t_parts, split(o_ii)))
    return inverse, as_columns(t_h) - dot_parts(t_parts, split(as_columns(o_h)))


def apply_gain(inverse, jump, t_ii, o_ri):
    g = dot3(o_ri, inverse)
    gt = dot3(g, t_ii)
    change = dot3(g, jump)
    short = -change.shape[0] % 128
    if short:
        change = jnp.concatenate([change, jnp.zeros((short, 128), jnp.float32)], axis=0)
    return g, gt, change.T[0:1, :]


def ordered(flag, mine, other):
    return jnp.concatenate(
        [jnp.where(flag, mine, other), jnp.where(flag, other, mine)], axis=0
    )


def kernel1(flags, own, other, h, other_h, re, ri, ie, ii, h_out):
    left, low = flags[0] == 1, flags[1] == 1
    s = own.shape[0] // 4
    e = 3 * s
    g, gt, change = gain(
        other[:, e:], own[e:, e:], own[:e, e:], other_h[...], h[:, e:]
    )
    mine = own[:e, :e] + dot3(gt, own[e:, :e])
    cross = -dot3(g, other[:, :e])
    h_new = h[:, :e] - change
    lefts = jnp.where(left, mine, cross)
    rights = jnp.where(left, cross, mine)

    def col(block, k):
        return block[:, k * s : (k + 1) * s]

    def rows(block):
        x, south, north = block[:s], block[s : 2 * s], block[2 * s :]
        return x, jnp.where(low, south, north), jnp.where(low, north, south)

    def put(k, side):
        x, y, i = rows(side)
        re[0:s, k * s : (k + 1) * s] = x
        re[s : 2 * s, k * s : (k + 1) * s] = y
        ie[:, k * s : (k + 1) * s] = i

    def put_i(k, side):
        x, y, i = rows(side)
        ri[0:s, k * s : (k + 1) * s] = x
        ri[s : 2 * s, k * s : (k + 1) * s] = y
        ii[0:s, k * s : (k + 1) * s] = i

    put(0, col(lefts, 0))
    put(1, col(rights, 0))
    for k, side in enumerate((lefts, rights)):
        put(2 + k, jnp.where(low, col(side, 1), col(side, 2)))
        put_i(k, jnp.where(low, col(side, 2), col(side, 1)))
    hx, hs, hn = col(h_new, 0), col(h_new, 1), col(h_new, 2)
    h_out[:, 0:s] = hx
    h_out[:, s : 2 * s] = jnp.where(low, hs, hn)
    hi = jnp.where(low, hn, hs)
    ii[s:, :] = jnp.broadcast_to(jnp.concatenate([hi, hi], axis=1), (8, 2 * s))


def gain2(flags, mine, mine_o, t, t_o, ri, h, g, gt, h_out):
    left = flags[0] == 1
    s = mine.shape[0] - 8

    def both(a, b):
        rows = ordered(left, a[0:s, :], b[0:s, :])
        ha, hb = a[s : s + 1, 0:s], b[s : s + 1, 0:s]
        vec = jnp.concatenate(
            [jnp.where(left, ha, hb), jnp.where(left, hb, ha)], axis=1
        )
        return rows, vec

    o_ii, o_h = both(mine, mine_o)
    t_ii, t_h = both(t, t_o)
    g[...], gt[...], change = gain(t_ii, o_ii, ri[...], t_h, o_h)
    h_out[...] = h[...] - change


def apply2(flags, re, g, gt, mine, mine_o, t, t_o, ext):
    left, low, first = flags[0] == 1, flags[1] == 1, flags[2] == 1
    s = mine.shape[0]
    own = re[...] + dot3(gt[...], ordered(left, mine[...], mine_o[...]))
    cross = -dot3(g[...], ordered(left, t[...], t_o[...]))
    lows = jnp.where(low, own, cross)
    ups = jnp.where(low, cross, own)
    west = jnp.concatenate([lows[:, :s], ups[:, :s]], axis=1)
    east = jnp.concatenate([lows[:, s : 2 * s], ups[:, s : 2 * s]], axis=1)
    ext[:, : 2 * s] = jnp.where(first, west, east)
    ext[:, 2 * s : 4 * s] = lows[:, 2 * s :]
    ext[:, 4 * s : 6 * s] = ups[:, 2 * s :]
    ext[:, 6 * s :] = jnp.where(first, east, west)


def quads(flags, v, beside, far, far_beside, near, last, part):
    left, low = flags[0] == 1, flags[1] == 1
    n = v.shape[0]
    other = [near[0:n], near[n : 2 * n], near[2 * n : 3 * n], last[...]]
    a, b, c, d = [
        part(left, mine, theirs)
        for mine, theirs in zip((v[...], beside[...], far[...], far_beside[...]), other)
    ]
    axis = 0 if a.shape[0] > 1 else 1

    def stack(one, two):
        return jnp.concatenate(
            [jnp.where(low, one, two), jnp.where(low, two, one)], axis=axis
        )

    return stack(a, b), stack(c, d)


def gain3(flags, v, beside, far, far_beside, near, last, rows, g, gt, change):
    n = v.shape[0] - 8
    e = 12 * n
    pieces = (v, beside, far, far_beside, near, last)
    o_ii, t_ii = quads(
        flags, *pieces, lambda left, a, b: ordered(left, a[0:n, e:], b[0:n, e:])
    )
    o_h, t_h = quads(flags, *pieces, lambda left, a, b: a[n : n + 1, 0 : 2 * n])
    g[...], gt[...], change[...] = gain(t_ii, o_ii, rows[:, e:], t_h, o_h)


def apply3(scale, flags, v, beside, far, far_beside, near, last, rows, g, gt, out):
    first = flags[2] == 1
    n = v.shape[0] - 8
    e = 12 * n
    pieces = (v, beside, far, far_beside, near, last)
    o_ie, t_ie = quads(
        flags, *pieces, lambda left, a, b: ordered(left, a[0:n, :e], b[0:n, :e])
    )
    own = (rows[:, :e] + dot3(gt[...], o_ie)) * scale
    cross = dot3(g[...], t_ie) * (-scale)
    out[:, :e] = jnp.where(first, own, cross)
    out[:, e:] = jnp.where(first, cross, own)


def call(body, flags, operands, shapes, flops):
    outs = [jax.ShapeDtypeStruct(shape, jnp.float32) for shape in shapes]
    moved = 4 * sum(math.prod(a.shape) for a in list(operands) + outs)
    return pl.pallas_call(
        body,
        out_shape=outs,
        in_specs=[pl.BlockSpec(memory_space=pltpu.SMEM)]
        + [pl.BlockSpec(memory_space=pltpu.VMEM)] * len(operands),
        out_specs=[pl.BlockSpec(memory_space=pltpu.VMEM)] * len(outs),
        compiler_params=pltpu.CompilerParams(vmem_limit_bytes=40 * 2**20),
        cost_estimate=pl.CostEstimate(flops=flops, bytes_accessed=moved, transcendentals=0),
    )(flags, *operands)


def from_behind(block, axis, distance):
    devices = range(lax.axis_size(axis))
    route = [(i - distance, i) for i in devices if i - distance in devices]
    return lax.ppermute(block, axis, route)


def partner(value, axis, distance):
    mask = 2**distance
    pairs = [(source, source ^ mask) for source in range(lax.axis_size(axis))]
    return lax.ppermute(value, axis, pairs)


def after(value, earlier):
    return lax.optimization_barrier((value, earlier))[0]


def send(value, moves):
    wide, high = lax.axis_size("gx"), lax.axis_size("gy")
    pairs = []
    for i in range(wide):
        for j in range(high):
            to = moves(i, j)
            if to is not None:
                pairs.append((i * high + j, to[0] * high + to[1]))
    return lax.ppermute(value, ("gx", "gy"), pairs)


def local(leaf_map, source_trace, tile_class, absorb_table):
    leaf_op = leaf_map[0, 0]
    s = leaf_op.shape[0] // 4
    classes = tile_class[0, 0]
    chosen = (
        classes[:, None] == jnp.arange(absorb_table.shape[0], dtype=jnp.int32)[None, :]
    ).astype(jnp.float32)
    levels = jnp.sum(chosen * absorb_table[None, :], axis=1)
    seg_width = leaf_op.shape[0] // classes.shape[0]
    spread = jnp.broadcast_to(levels[:, None], (classes.shape[0], seg_width)).reshape(-1)
    leaf_h = spread * source_trace[0, 0]
    column = lax.axis_index("gx")
    row_index = lax.axis_index("gy")
    left = column % 2 == 0
    low = row_index % 2 == 0
    first = column // 2 % 2 == 0
    flags = jnp.stack([left, low, first]).astype(jnp.int32)

    def sides(a, axis):
        w, e, so, no = jnp.split(a, 4, axis=axis)
        x, i = jnp.where(left, w, e), jnp.where(left, e, w)
        return jnp.concatenate([x, so, no, i], axis=axis)

    own = sides(sides(leaf_op, 0), 1)
    h = sides(leaf_h, 0)[None]
    other, other_h = partner((own[3 * s :], h[:, 3 * s :]), "gx", 0)
    re, ri, ie, ii, h = call(
        kernel1,
        flags,
        [own, other, h, other_h],
        [(2 * s, 4 * s), (2 * s, 2 * s), (s, 4 * s), (s + 8, 2 * s), (1, 2 * s)],
        6 * s**3 * 50,
    )

    t_ii = partner(ii, "gy", 0)
    ii_o = partner(ii, "gx", 0)
    t_ii_o = partner(t_ii, "gx", 0)
    t_ie = partner(after(ie, t_ii), "gy", 0)
    ie_o = partner(ie, "gx", 0)
    t_ie_o = partner(t_ie, "gx", 0)
    g, gt, h = call(
        gain2,
        flags,
        [ii, ii_o, t_ii, t_ii_o, ri, h],
        [(2 * s, 2 * s), (2 * s, 2 * s), (1, 2 * s)],
        6 * (2 * s) ** 3 * 20,
    )
    (merged,) = call(
        apply2,
        flags,
        [re, g, gt, ie, ie_o, t_ie, t_ie_o],
        [(2 * s, 8 * s)],
        6 * (2 * s) ** 2 * 8 * s,
    )

    half = s // 2
    x, y, h_x, h_y = merged[:s], merged[s:], h[:, :s], h[:, s:]

    def pack(rows, vector):
        row = jnp.pad(vector, ((0, 0), (0, 7 * s)))
        return jnp.concatenate([rows, jnp.broadcast_to(row, (8, 8 * s))], axis=0)

    holder = left != first

    def give(i, j):
        return (i ^ 1, j) if (i % 2 == 0) != (i // 2 % 2 == 0) else None

    got = send(pack(jnp.where(left, x[half:], x[:half]), h_x), give)
    v = jnp.where(holder, pack(jnp.where(left, x[:half], x[half:]), h_x), got)
    beside = partner(v, "gy", 0)
    far = partner(v, "gx", 1)
    far_beside = partner(beside, "gx", 1)
    near = partner(jnp.concatenate([v, beside, far], axis=0), "gx", 0)
    last = partner(far_beside, "gx", 0)
    pieces = [v, beside, far, far_beside, near, last]

    def in_first(i):
        return i // 2 % 2 == 0

    def move_a(i, j):
        if i % 2 == 0 and j % 2 == 0:
            return (i, j + 1)
        if i % 2 == 1 and j % 2 == 0 and not in_first(i):
            return (i - 1, j)
        return None

    def move_b(i, j):
        if j % 2 == 1 and i % 2 == (0 if in_first(i) else 1):
            return (i - i % 2, j - 1)
        return None

    def move_c(i, j):
        return (i + 1, j - 1) if i % 2 == 0 and j % 2 == 1 else None

    def move_d(i, j):
        if j % 2 == 1 and (i % 2 == 0 or not in_first(i)):
            return (i ^ 1, j)
        return None

    got_a = send(jnp.where(left, pack(y, h_y), pack(x, h_x)), move_a)
    got_b = send(pack(x[:half], h_x), move_b)
    got_c = send(pack(y[:half], h_y), move_c)
    got_d = send(
        jnp.where(left, pack(y[half:], h_y), pack(x[half:], h_x)), move_d
    )

    def assemble(x, y, a, b, c, d):
        lower = jnp.where(
            left,
            jnp.concatenate([jnp.where(first, x, a), b], axis=0),
            jnp.concatenate([y, c], axis=0),
        )
        upper = jnp.where(
            left,
            jnp.concatenate([jnp.where(first, x[half:], d), a], axis=0),
            jnp.concatenate([d, y], axis=0),
        )
        return jnp.where(low, lower, upper)

    rows = assemble(x, y, got_a[:s], got_b[:half], got_c[:half], got_d[:half])
    row_h = assemble(
        h_x[0],
        h_y[0],
        got_a[s, :s],
        got_b[half, :half],
        got_c[half, :half],
        got_d[half, half:s],
    )
    rows_dev = 3 * s // 2
    g, gt, change = call(
        gain3,
        flags,
        [*pieces, rows],
        [(rows_dev, 2 * s), (rows_dev, 2 * s), (1, 2 * s)],
        6 * (2 * s) ** 3 * 20,
    )
    h3 = row_h - change[0, :rows_dev]
    scale = math.sqrt(12 * s)
    (scaled,) = call(
        functools.partial(apply3, scale),
        flags,
        [*pieces, rows, g, gt],
        [(rows_dev, 12 * s)],
        6 * rows_dev * 2 * s * 12 * s,
    )

    top_h = h3
    for flag, axis, distance in ((low, "gy", 0), (left, "gx", 0), (first, "gx", 1)):
        top_h = ordered(flag, top_h, partner(top_h, axis, distance))
    edge = 2 * s
    blocks = [top_h[k * edge : (k + 1) * edge] for k in range(6)]
    from_west = from_behind(blocks[3], "gx", 4)
    from_east = from_behind(blocks[0], "gx", -4)
    from_south = from_behind(jnp.concatenate([blocks[2], blocks[5]]), "gy", 2)
    from_north = from_behind(jnp.concatenate([blocks[1], blocks[4]]), "gy", -2)
    from_west, from_east, from_south, from_north = lax.optimization_barrier(
        (from_west, from_east, from_south, from_north)
    )
    incoming = -jnp.concatenate(
        [
            from_west,
            from_south[:edge],
            from_north[:edge],
            from_east,
            from_south[edge:],
            from_north[edge:],
        ]
    )
    out_rows = jnp.sum(scaled * (incoming / scale)[None, :], axis=1) + h3
    return (scaled[None, None], out_rows[None, None])


def solution(mesh):
    return jax.shard_map(
        local,
        mesh=mesh,
        in_specs=(P("gx", "gy", None, None), P("gx", "gy", None), P("gx", "gy", None), P()),
        out_specs=(P("gx", "gy", None, None), P("gx", "gy", None)),
        check_vma=False,
    )
```

```python
import functools
import math

import jax
import jax.numpy as jnp
from jax import lax
from jax.experimental import pallas as pl
from jax.experimental.pallas import tpu as pltpu
from jax.sharding import PartitionSpec as P

DOUBLINGS = 9


def split(value):
    high = value.astype(jnp.bfloat16)
    low = (value - high.astype(jnp.float32)).astype(jnp.bfloat16)
    return high, low


def dot_parts(left, right):
    dot = functools.partial(jnp.dot, preferred_element_type=jnp.float32)
    return dot(left[0], right[0]) + (dot(left[0], right[1]) + dot(left[1], right[0]))


def dot3(left, right):
    return dot_parts(split(left), split(right))


def resolvent(product):
    size = product.shape[0]
    rows = lax.broadcasted_iota(jnp.int32, (size, size), 0)
    cols = lax.broadcasted_iota(jnp.int32, (size, size), 1)
    total = jnp.where(rows == cols, 1.0, 0.0) + product
    parts = split(product)
    power = dot_parts(parts, parts)
    for step in range(1, DOUBLINGS):
        parts = split(power)
        if step < DOUBLINGS - 1:
            sums = split(total)
            both = tuple(jnp.concatenate([s, p], axis=0) for s, p in zip(sums, parts))
            out = dot_parts(both, parts)
            total = total + out[:size]
            power = out[size:]
        else:
            total = total + dot_parts(split(total), parts)
    return total


def as_columns(row):
    return jnp.broadcast_to(row, (128, row.shape[1])).T


def gain(t_ii, o_ii, o_ri, t_h, o_h):
    return apply_gain(*interface(t_ii, o_ii, t_h, o_h), t_ii, o_ri)


def interface(t_ii, o_ii, t_h, o_h):
    t_parts = split(t_ii)
    inverse = resolvent(dot_parts(t_parts, split(o_ii)))
    return inverse, as_columns(t_h) - dot_parts(t_parts, split(as_columns(o_h)))


def apply_gain(inverse, jump, t_ii, o_ri):
    g = dot3(o_ri, inverse)
    gt = dot3(g, t_ii)
    change = dot3(g, jump)
    short = -change.shape[0] % 128
    if short:
        change = jnp.concatenate([change, jnp.zeros((short, 128), jnp.float32)], axis=0)
    return g, gt, change.T[0:1, :]


def ordered(flag, mine, other):
    return jnp.concatenate(
        [jnp.where(flag, mine, other), jnp.where(flag, other, mine)], axis=0
    )


def kernel1(flags, own, other, h, other_h, re, ri, ie, ii, h_out):
    left, low = flags[0] == 1, flags[1] == 1
    s = own.shape[0] // 4
    e = 3 * s
    g, gt, change = gain(
        other[:, e:], own[e:, e:], own[:e, e:], other_h[...], h[:, e:]
    )
    mine = own[:e, :e] + dot3(gt, own[e:, :e])
    cross = -dot3(g, other[:, :e])
    h_new = h[:, :e] - change
    lefts = jnp.where(left, mine, cross)
    rights = jnp.where(left, cross, mine)

    def col(block, k):
        return block[:, k * s : (k + 1) * s]

    def rows(block):
        x, south, north = block[:s], block[s : 2 * s], block[2 * s :]
        return x, jnp.where(low, south, north), jnp.where(low, north, south)

    def put(k, side):
        x, y, i = rows(side)
        re[0:s, k * s : (k + 1) * s] = x
        re[s : 2 * s, k * s : (k + 1) * s] = y
        ie[:, k * s : (k + 1) * s] = i

    def put_i(k, side):
        x, y, i = rows(side)
        ri[0:s, k * s : (k + 1) * s] = x
        ri[s : 2 * s, k * s : (k + 1) * s] = y
        ii[0:s, k * s : (k + 1) * s] = i

    put(0, col(lefts, 0))
    put(1, col(rights, 0))
    for k, side in enumerate((lefts, rights)):
        put(2 + k, jnp.where(low, col(side, 1), col(side, 2)))
        put_i(k, jnp.where(low, col(side, 2), col(side, 1)))
    hx, hs, hn = col(h_new, 0), col(h_new, 1), col(h_new, 2)
    h_out[:, 0:s] = hx
    h_out[:, s : 2 * s] = jnp.where(low, hs, hn)
    hi = jnp.where(low, hn, hs)
    ii[s:, :] = jnp.broadcast_to(jnp.concatenate([hi, hi], axis=1), (8, 2 * s))


def gain2(flags, mine, mine_o, t, t_o, ri, h, g, gt, h_out):
    left = flags[0] == 1
    s = mine.shape[0] - 8

    def both(a, b):
        rows = ordered(left, a[0:s, :], b[0:s, :])
        ha, hb = a[s : s + 1, 0:s], b[s : s + 1, 0:s]
        vec = jnp.concatenate(
            [jnp.where(left, ha, hb), jnp.where(left, hb, ha)], axis=1
        )
        return rows, vec

    o_ii, o_h = both(mine, mine_o)
    t_ii, t_h = both(t, t_o)
    g[...], gt[...], change = gain(t_ii, o_ii, ri[...], t_h, o_h)
    h_out[...] = h[...] - change


def apply2(flags, re, g, gt, mine, mine_o, t, t_o, ext):
    left, low, first = flags[0] == 1, flags[1] == 1, flags[2] == 1
    s = mine.shape[0]
    own = re[...] + dot3(gt[...], ordered(left, mine[...], mine_o[...]))
    cross = -dot3(g[...], ordered(left, t[...], t_o[...]))
    lows = jnp.where(low, own, cross)
    ups = jnp.where(low, cross, own)
    west = jnp.concatenate([lows[:, :s], ups[:, :s]], axis=1)
    east = jnp.concatenate([lows[:, s : 2 * s], ups[:, s : 2 * s]], axis=1)
    ext[:, : 2 * s] = jnp.where(first, west, east)
    ext[:, 2 * s : 4 * s] = lows[:, 2 * s :]
    ext[:, 4 * s : 6 * s] = ups[:, 2 * s :]
    ext[:, 6 * s :] = jnp.where(first, east, west)


def quads(flags, v, beside, far, far_beside, near, last, part):
    left, low = flags[0] == 1, flags[1] == 1
    n = v.shape[0]
    other = [near[0:n], near[n : 2 * n], near[2 * n : 3 * n], last[...]]
    a, b, c, d = [
        part(left, mine, theirs)
        for mine, theirs in zip((v[...], beside[...], far[...], far_beside[...]), other)
    ]
    axis = 0 if a.shape[0] > 1 else 1

    def stack(one, two):
        return jnp.concatenate(
            [jnp.where(low, one, two), jnp.where(low, two, one)], axis=axis
        )

    return stack(a, b), stack(c, d)


def gain3(flags, v, beside, far, far_beside, near, last, rows, g, gt, change):
    n = v.shape[0] - 8
    e = 12 * n
    pieces = (v, beside, far, far_beside, near, last)
    o_ii, t_ii = quads(
        flags, *pieces, lambda left, a, b: ordered(left, a[0:n, e:], b[0:n, e:])
    )
    o_h, t_h = quads(flags, *pieces, lambda left, a, b: a[n : n + 1, 0 : 2 * n])
    g[...], gt[...], change[...] = gain(t_ii, o_ii, rows[:, e:], t_h, o_h)


def apply3(scale, flags, v, beside, far, far_beside, near, last, rows, g, gt, out):
    first = flags[2] == 1
    n = v.shape[0] - 8
    e = 12 * n
    pieces = (v, beside, far, far_beside, near, last)
    o_ie, t_ie = quads(
        flags, *pieces, lambda left, a, b: ordered(left, a[0:n, :e], b[0:n, :e])
    )
    own = (rows[:, :e] + dot3(gt[...], o_ie)) * scale
    cross = dot3(g[...], t_ie) * (-scale)
    out[:, :e] = jnp.where(first, own, cross)
    out[:, e:] = jnp.where(first, cross, own)


def call(body, flags, operands, shapes, flops):
    outs = [jax.ShapeDtypeStruct(shape, jnp.float32) for shape in shapes]
    moved = 4 * sum(math.prod(a.shape) for a in list(operands) + outs)
    return pl.pallas_call(
        body,
        out_shape=outs,
        in_specs=[pl.BlockSpec(memory_space=pltpu.SMEM)]
        + [pl.BlockSpec(memory_space=pltpu.VMEM)] * len(operands),
        out_specs=[pl.BlockSpec(memory_space=pltpu.VMEM)] * len(outs),
        compiler_params=pltpu.CompilerParams(vmem_limit_bytes=40 * 2**20),
        cost_estimate=pl.CostEstimate(flops=flops, bytes_accessed=moved, transcendentals=0),
    )(flags, *operands)


def from_behind(block, axis, distance):
    devices = range(lax.axis_size(axis))
    route = [(i - distance, i) for i in devices if i - distance in devices]
    return lax.ppermute(block, axis, route)


def partner(value, axis, distance):
    mask = 2**distance
    pairs = [(source, source ^ mask) for source in range(lax.axis_size(axis))]
    return lax.ppermute(value, axis, pairs)


def after(value, earlier):
    return lax.optimization_barrier((value, earlier))[0]


def send(value, moves):
    wide, high = lax.axis_size("gx"), lax.axis_size("gy")
    pairs = []
    for i in range(wide):
        for j in range(high):
            to = moves(i, j)
            if to is not None:
                pairs.append((i * high + j, to[0] * high + to[1]))
    return lax.ppermute(value, ("gx", "gy"), pairs)


def local(leaf_map, source_trace, tile_class, absorb_table):
    leaf_op = leaf_map[0, 0]
    s = leaf_op.shape[0] // 4
    classes = tile_class[0, 0]
    chosen = (
        classes[:, None] == jnp.arange(absorb_table.shape[0], dtype=jnp.int32)[None, :]
    ).astype(jnp.float32)
    levels = jnp.sum(chosen * absorb_table[None, :], axis=1)
    seg_width = leaf_op.shape[0] // classes.shape[0]
    spread = jnp.broadcast_to(levels[:, None], (classes.shape[0], seg_width)).reshape(-1)
    leaf_h = spread * source_trace[0, 0]
    column = lax.axis_index("gx")
    row_index = lax.axis_index("gy")
    left = column % 2 == 0
    low = row_index % 2 == 0
    first = column // 2 % 2 == 0
    flags = jnp.stack([left, low, first]).astype(jnp.int32)

    def sides(a, axis):
        w, e, so, no = jnp.split(a, 4, axis=axis)
        x, i = jnp.where(left, w, e), jnp.where(left, e, w)
        return jnp.concatenate([x, so, no, i], axis=axis)

    own = sides(sides(leaf_op, 0), 1)
    h = sides(leaf_h, 0)[None]
    other, other_h = partner((own[3 * s :], h[:, 3 * s :]), "gx", 0)
    re, ri, ie, ii, h = call(
        kernel1,
        flags,
        [own, other, h, other_h],
        [(2 * s, 4 * s), (2 * s, 2 * s), (s, 4 * s), (s + 8, 2 * s), (1, 2 * s)],
        6 * s**3 * 50,
    )

    t_ii = partner(ii, "gy", 0)
    ii_o = partner(ii, "gx", 0)
    t_ii_o = partner(t_ii, "gx", 0)
    t_ie = partner(after(ie, t_ii), "gy", 0)
    ie_o = partner(ie, "gx", 0)
    g, gt, h = call(
        gain2,
        flags,
        [ii, ii_o, t_ii, t_ii_o, ri, h],
        [(2 * s, 2 * s), (2 * s, 2 * s), (1, 2 * s)],
        6 * (2 * s) ** 3 * 20,
    )
    t_ie_o = partner(after(t_ie, g), "gx", 0)
    (merged,) = call(
        apply2,
        flags,
        [re, g, gt, ie, ie_o, t_ie, t_ie_o],
        [(2 * s, 8 * s)],
        6 * (2 * s) ** 2 * 8 * s,
    )

    half = s // 2
    x, y, h_x, h_y = merged[:s], merged[s:], h[:, :s], h[:, s:]

    def pack(rows, vector):
        row = jnp.pad(vector, ((0, 0), (0, 7 * s)))
        return jnp.concatenate([rows, jnp.broadcast_to(row, (8, 8 * s))], axis=0)

    holder = left != first

    def give(i, j):
        return (i ^ 1, j) if (i % 2 == 0) != (i // 2 % 2 == 0) else None

    got = send(pack(jnp.where(left, x[half:], x[:half]), h_x), give)
    v = jnp.where(holder, pack(jnp.where(left, x[:half], x[half:]), h_x), got)
    beside = partner(v, "gy", 0)
    far = partner(v, "gx", 1)
    far_beside = partner(beside, "gx", 1)
    near = partner(jnp.concatenate([v, beside, far], axis=0), "gx", 0)
    last = partner(far_beside, "gx", 0)
    pieces = [v, beside, far, far_beside, near, last]

    def in_first(i):
        return i // 2 % 2 == 0

    def move_a(i, j):
        if i % 2 == 0 and j % 2 == 0:
            return (i, j + 1)
        if i % 2 == 1 and j % 2 == 0 and not in_first(i):
            return (i - 1, j)
        return None

    def move_b(i, j):
        if j % 2 == 1 and i % 2 == (0 if in_first(i) else 1):
            return (i - i % 2, j - 1)
        return None

    def move_c(i, j):
        return (i + 1, j - 1) if i % 2 == 0 and j % 2 == 1 else None

    def move_d(i, j):
        if j % 2 == 1 and (i % 2 == 0 or not in_first(i)):
            return (i ^ 1, j)
        return None

    got_a = send(jnp.where(left, pack(y, h_y), pack(x, h_x)), move_a)
    got_b = send(pack(x[:half], h_x), move_b)
    got_c = send(pack(y[:half], h_y), move_c)
    got_d = send(
        jnp.where(left, pack(y[half:], h_y), pack(x[half:], h_x)), move_d
    )

    def assemble(x, y, a, b, c, d):
        lower = jnp.where(
            left,
            jnp.concatenate([jnp.where(first, x, a), b], axis=0),
            jnp.concatenate([y, c], axis=0),
        )
        upper = jnp.where(
            left,
            jnp.concatenate([jnp.where(first, x[half:], d), a], axis=0),
            jnp.concatenate([d, y], axis=0),
        )
        return jnp.where(low, lower, upper)

    rows = assemble(x, y, got_a[:s], got_b[:half], got_c[:half], got_d[:half])
    row_h = assemble(
        h_x[0],
        h_y[0],
        got_a[s, :s],
        got_b[half, :half],
        got_c[half, :half],
        got_d[half, half:s],
    )
    rows_dev = 3 * s // 2
    g, gt, change = call(
        gain3,
        flags,
        [*pieces, rows],
        [(rows_dev, 2 * s), (rows_dev, 2 * s), (1, 2 * s)],
        6 * (2 * s) ** 3 * 20,
    )
    h3 = row_h - change[0, :rows_dev]
    scale = math.sqrt(12 * s)
    (scaled,) = call(
        functools.partial(apply3, scale),
        flags,
        [*pieces, rows, g, gt],
        [(rows_dev, 12 * s)],
        6 * rows_dev * 2 * s * 12 * s,
    )

    top_h = h3
    for flag, axis, distance in ((low, "gy", 0), (left, "gx", 0), (first, "gx", 1)):
        top_h = ordered(flag, top_h, partner(top_h, axis, distance))
    edge = 2 * s
    blocks = [top_h[k * edge : (k + 1) * edge] for k in range(6)]
    from_west = from_behind(blocks[3], "gx", 4)
    from_east = from_behind(blocks[0], "gx", -4)
    from_south = from_behind(jnp.concatenate([blocks[2], blocks[5]]), "gy", 2)
    from_north = from_behind(jnp.concatenate([blocks[1], blocks[4]]), "gy", -2)
    from_west, from_east, from_south, from_north = lax.optimization_barrier(
        (from_west, from_east, from_south, from_north)
    )
    incoming = -jnp.concatenate(
        [
            from_west,
            from_south[:edge],
            from_north[:edge],
            from_east,
            from_south[edge:],
            from_north[edge:],
        ]
    )
    out_rows = jnp.sum(scaled * (incoming / scale)[None, :], axis=1) + h3
    return (scaled[None, None], out_rows[None, None])


def solution(mesh):
    return jax.shard_map(
        local,
        mesh=mesh,
        in_specs=(P("gx", "gy", None, None), P("gx", "gy", None), P("gx", "gy", None), P()),
        out_specs=(P("gx", "gy", None, None), P("gx", "gy", None)),
        check_vma=False,
    )
```
